128 devices in a mesh: aux: 4 (over x_hi, core), row: 32 (over z, x_lo, y).
Axes of the slice: x: 4 (x_hi: 2, x_lo: 2; x = x_hi * 2 + x_lo), y: 4, z: 4, core: 2. Of those that a mesh axis runs over, the one named last changes fastest.
Arguments:
- slab: bfloat16 [20, 8192, 8192], P('aux', 'row'), may hold values from -6 to 6
- screen: int32 [4, 64, 64], P('aux', 'row'), may hold values 0 or 1
- orbitals: bfloat16 [8192, 128], P('row'), may hold values from -0.0625 to 0.0625
- hcore: float32 [8192, 8192], P('row', 'aux'), may hold values from -6 to 6
Outputs:
- exchange: float32 [8192, 8192], P('row', 'aux')
- gradient: float32 [8192, 128], P('row')
The draws below stay inside these ranges and needn't reach their ends.
All inputs are finite; a program needn't handle non-finite values. No bound on the sum of `screen` on one device may be relied on, other than what follows from the above.
Results may differ from the reference program's by a relative error of at most 0.0035.
Values may be sent and summed in bfloat16 or wider, within the bound.
No kernel may reach another device: no remote copies, remote signals or barrier semaphores. Data moves between devices by JAX's collectives and lax.ppermute only.
A program may use at most 128 MiB of HBM per device.

```python
import math
import jax
import jax.numpy as jnp
from jax import lax

NAO = 8192
OCCUPIED_COUNT = 128
BLOCK = 128
QD = 5
AUXILIARY_TOTAL = 20
NBLK = 64
N_AUX = 4


def plant(drawn, stream_key, low, top_value):
    dims = drawn.shape
    spot = [jax.random.randint(jax.random.fold_in(stream_key, axis), (), 0, dims[axis]) for axis in range(len(dims))]
    drawn = drawn.at[tuple(spot)].set(low)
    longest = dims.index(max(dims))
    spot[longest] = (spot[longest] + 1) % dims[longest]
    return drawn.at[tuple(spot)].set(top_value)


def block_levels(stream_key, dims, split, low, largest):
    def one(position, blocks):
        heights = jax.random.uniform(jax.random.fold_in(jax.random.fold_in(stream_key, 6), position), (blocks,), jnp.float32, low / len(split), largest / len(split))
        return jnp.repeat(jnp.exp(heights), dims[position] // blocks).reshape((-1,) + (1,) * (len(dims) - position - 1))

    level = one(*split[0])
    for cut in split[1:]:
        level = level * one(*cut)
    return level


def noise(own_key, extent, deviation, most, shards=(), kind=jnp.bfloat16):
    values = jax.random.normal(own_key, extent, jnp.float32) * deviation
    if len(shards) > 0:
        values = block_levels(own_key, extent, shards, -0.22, 0.18) * values
    return jnp.clip(values, min=-most, max=most).astype(kind)


def setup_inputs(seed: int = 0) -> dict:
    key_of = jax.random.split(jax.random.key(seed), 5)
    slab = noise(key_of[0], (AUXILIARY_TOTAL, NAO, NAO), 1.0, 6.0, ((0, 4), (1, 32)))
    screen = plant((jax.random.randint(key_of[1], (N_AUX, NBLK, NBLK), 0, 4) < 3).astype(jnp.int32), jax.random.fold_in(key_of[1], 1), 0, 1)
    orbitals = noise(key_of[2], (NAO, OCCUPIED_COUNT), NAO ** -0.5, 0.0625, ((0, 32),))
    hcore = noise(key_of[3], (NAO, NAO), 1.0, 6.0, ((0, 32), (1, 4)), jnp.float32)
    return dict(slab=slab, screen=screen, orbitals=orbitals, hcore=hcore)


def reference(slab, screen, orbitals, hcore):

    def transform_one(aux_index):
        group_index = aux_index // QD
        tile_mask = jnp.repeat(jnp.repeat(screen[group_index], BLOCK, axis=0), BLOCK, axis=1)
        masked = slab[aux_index] * tile_mask.astype(jnp.bfloat16)
        return jnp.dot(masked, orbitals, preferred_element_type=jnp.float32).astype(jnp.bfloat16)
    half_slab = lax.map(transform_one, jnp.arange(AUXILIARY_TOTAL, dtype=jnp.int32))
    flat_integrals = jnp.transpose(half_slab, (1, 0, 2)).reshape(NAO, AUXILIARY_TOTAL * OCCUPIED_COUNT)
    exchange_scale = 1.0 / math.sqrt(AUXILIARY_TOTAL * OCCUPIED_COUNT)
    exchange = jnp.dot(flat_integrals, flat_integrals.T, preferred_element_type=jnp.float32) * exchange_scale
    fock_bf = (hcore - 0.5 * exchange).astype(jnp.bfloat16)
    applied = jnp.dot(fock_bf, orbitals, preferred_element_type=jnp.float32)
    orbit_rows = orbitals.astype(jnp.float32)
    projection = jnp.dot(orbit_rows.T, applied, precision=lax.Precision.HIGHEST)
    gradient = applied - jnp.dot(orbit_rows, projection, precision=lax.Precision.HIGHEST)
    return (exchange, gradient)
```

```python
import math

import jax
import jax.numpy as jnp
from jax import lax
from jax.sharding import Mesh, PartitionSpec as P

ROW = ("z", "xl", "y")
AUX = ("xh", "core")
PLANE = ("xl", "y")
BF = jnp.bfloat16
F32 = jnp.float32


def flip(value, axis, mask, size):
    return lax.ppermute(value, axis, [(k, k ^ mask) for k in range(size)])


def shift(value, axis, step, size):
    return lax.ppermute(value, axis, [(k, (k + step) % size) for k in range(size)])


def two_term(value):
    high = lax.reduce_precision(value, 8, 7)
    return high.astype(BF), (value - high).astype(BF)


def on_device(slab, screen, orbitals, hcore):
    quantity, row_count, basis = slab.shape
    occupied = orbitals.shape[1]
    core = lax.axis_index("core")
    aux = lax.axis_index(AUX)
    z = lax.axis_index("z")
    plane = lax.axis_index(PLANE)
    row_devices = lax.axis_size(ROW)
    scale = 1.0 / math.sqrt(quantity * 4 * occupied)

    halves = orbitals.reshape(2, row_count // 2, occupied)
    own = lax.dynamic_index_in_dim(halves, core, 0, keepdims=False)
    mine = lax.all_to_all(
        jnp.broadcast_to(own[None], (row_devices,) + own.shape), ROW, 0, 0, tiled=True
    )
    other = flip(mine, "core", 1, 2)
    first = jnp.where(core == 0, mine, other)
    second = jnp.where(core == 0, other, mine)
    everything = jnp.stack([first, second], axis=1)

    tile = basis // screen.shape[2]
    tiles = everything.reshape(screen.shape[2], tile, occupied)
    parts = []
    for t in range(screen.shape[1]):
        kept = (tiles * screen[0, t].astype(BF)[:, None, None]).reshape(basis, occupied)
        block = slab[:, t * tile : (t + 1) * tile, :]
        parts.append(
            jnp.einsum("qmn,ni->qmi", block, kept, preferred_element_type=F32).astype(BF)
        )
    half = jnp.concatenate(parts, axis=1)
    flat = jnp.transpose(half, (1, 0, 2)).reshape(row_count, quantity * occupied)
    depth = quantity * occupied

    swapped = lax.ppermute(
        flat, ("xh", "core", "z"), [(a * 4 + k, k * 4 + a) for a in range(4) for k in range(4)]
    )
    rows = [swapped] + [flip(swapped, AUX, m, 4) for m in (1, 2, 3)]
    rows = jnp.stack(rows)
    cols = jnp.zeros((8, row_count, depth), BF)
    cols = lax.dynamic_update_index_in_dim(cols, swapped, plane, 0)
    for m in range(1, 8):
        cols = lax.dynamic_update_index_in_dim(cols, flip(swapped, PLANE, m, 8), plane ^ m, 0)
    cols = cols.reshape(8 * row_count, depth)

    def product(step):
        block = lax.dynamic_index_in_dim(rows, ((z + step) % 4) ^ aux, 0, keepdims=False)
        return lax.dot_general(
            block, cols, (((1,), (1,)), ((), ())), preferred_element_type=F32
        )

    width = cols.shape[0] // 2
    far = product(2).astype(BF)
    far_a = shift(far[:, :width], "z", 1, 4)
    far_b = shift(far[:, width:], "z", -1, 4)
    up = product(1)
    down = product(3)
    up_b = shift(up[:, width:].astype(BF), "z", 1, 4)
    down_a = shift(down[:, :width].astype(BF), "z", -1, 4)
    up_a = shift((up[:, :width] + far_a.astype(F32)).astype(BF), "z", 1, 4)
    down_b = shift((down[:, width:] + far_b.astype(F32)).astype(BF), "z", -1, 4)
    home = product(0)
    left = home[:, :width] + up_a.astype(F32) + down_a.astype(F32)
    right = home[:, width:] + up_b.astype(F32) + down_b.astype(F32)
    exchange = jnp.concatenate([left, right], axis=1) * scale

    col_count = hcore.shape[1]
    column_orbitals = lax.dynamic_slice_in_dim(
        everything.reshape(basis, occupied), aux * col_count, col_count, 0
    )
    high, low = two_term(hcore)
    core_part = jnp.dot(high, column_orbitals, preferred_element_type=F32) + jnp.dot(
        low, column_orbitals, preferred_element_type=F32
    )
    orbit_rows = orbitals.astype(F32)
    core_projection = jnp.dot(orbit_rows.T, core_part, precision=lax.Precision.HIGHEST)
    overlap = lax.dot_general(
        flat, orbitals, (((0,), (0,)), ((), ())), preferred_element_type=F32
    )
    summed = jnp.concatenate([overlap, core_projection], axis=0)
    pieces = summed.reshape(row_devices, -1, occupied)
    piece = jnp.sum(lax.all_to_all(pieces, ROW, 0, 0, tiled=True), axis=0)
    summed = lax.all_to_all(
        jnp.broadcast_to(piece[None], pieces.shape), ROW, 0, 0, tiled=True
    ).reshape(summed.shape)
    overlap, core_projection = summed[:depth], summed[depth:]
    o_high, o_low = two_term(overlap)
    exchange_part = jnp.dot(flat, o_high, preferred_element_type=F32) + jnp.dot(
        flat, o_low, preferred_element_type=F32
    )
    applied = core_part - (0.5 * scale) * exchange_part
    projection = core_projection - (0.5 * scale) * jnp.dot(
        overlap.T, overlap, precision=lax.Precision.HIGHEST
    )
    both = jnp.concatenate([applied, projection], axis=0)
    both = both + flip(both, "core", 1, 2)
    both = both + flip(both, "xh", 1, 2)
    applied, projection = both[:row_count], both[row_count:]
    gradient = applied - jnp.dot(orbit_rows, projection, precision=lax.Precision.HIGHEST)
    return (exchange, gradient)


def solution(mesh):
    finer = Mesh(mesh.devices.reshape(2, 2, 4, 2, 4), AUX + ROW)
    in_specs = (P(AUX, ROW, None), P(AUX, ROW, None), P(ROW, None), P(ROW, AUX))
    out_specs = (P(ROW, AUX), P(ROW, None))
    return jax.shard_map(
        on_device, mesh=finer, in_specs=in_specs, out_specs=out_specs, check_vma=False
    )
```

```python
import functools
import math

import jax
import jax.numpy as jnp
from jax import lax
from jax.experimental import pallas as pl
from jax.experimental.pallas import tpu as pltpu
from jax.sharding import Mesh, PartitionSpec as P

ROW = ("z", "xl", "y")
AUX = ("xh", "core")
PLANE = ("xl", "y")
BF = jnp.bfloat16
F32 = jnp.float32
SHARDS = 8
VMEM_LIMIT = 16 * 1024 * 1024


def flip(value, axis, mask, size):
    return lax.ppermute(value, axis, [(k, k ^ mask) for k in range(size)])


def shift(value, axis, step, size):
    return lax.ppermute(value, axis, [(k, (k + step) % size) for k in range(size)])


def spot(s):
    return (s % 2) * 4 + s // 2


def two_term(value):
    high = lax.reduce_precision(value, 8, 7)
    return high.astype(BF), (value - high).astype(BF)


def screened(screen_ref, t, orbit_ref, parity, begin):
    return jnp.concatenate(
        [
            orbit_ref[v] * screen_ref[t, 2 * v + parity].astype(F32).astype(BF)
            for v in range(begin, begin + SHARDS)
        ],
        axis=0,
    )


def one_parity(parity, screen_ref, slab_ref, orbit_ref, t):
    quantity = slab_ref.shape[0]
    shards, tile, _ = orbit_ref.shape
    total = None
    for begin in range(0, shards, SHARDS):
        block = jnp.concatenate(
            [
                slab_ref[
                    :,
                    t * tile : (t + 1) * tile,
                    pl.ds(pl.multiple_of((2 * v + parity) * tile, tile), tile),
                ].reshape(quantity * tile, tile)
                for v in range(begin, begin + SHARDS)
            ],
            axis=1,
        )
        term = jnp.dot(
            block,
            screened(screen_ref, t, orbit_ref, parity, begin),
            preferred_element_type=F32,
        )
        total = term if total is None else total + term
    return total


def begin_kernel(parity_ref, screen_ref, slab_ref, orbit_ref, kept_ref, out_ref, sems):
    quantity, rows, _ = kept_ref.shape
    tile = orbit_ref.shape[1]
    groups = rows // tile
    copies = []
    for t in range(groups):
        for q in range(quantity):
            part = (q, pl.ds(t * tile, tile))
            copies.append(
                pltpu.make_async_copy(slab_ref.at[part], kept_ref.at[part], sems.at[t, q])
            )
            copies[-1].start()
    for t in range(groups):
        for q in range(quantity):
            copies[t * quantity + q].wait()
        out_ref[t] = one_parity(parity_ref[0], screen_ref, kept_ref, orbit_ref, t)


def end_kernel(parity_ref, screen_ref, kept_ref, orbit_ref, begun_ref, out_ref):
    quantity, rows, _ = kept_ref.shape
    tile = orbit_ref.shape[1]
    for t in range(rows // tile):
        total = begun_ref[t] + one_parity(parity_ref[0], screen_ref, kept_ref, orbit_ref, t)
        for q in range(quantity):
            out_ref[t * tile : (t + 1) * tile, q * tile : (q + 1) * tile] = total[
                q * tile : (q + 1) * tile
            ].astype(BF)


def half_begin(parity, screen, slab, orbit):
    quantity, rows, _ = slab.shape
    _, tile, occupied = orbit.shape
    groups = rows // tile
    vmem = pl.BlockSpec(memory_space=pltpu.VMEM)
    smem = pl.BlockSpec(memory_space=pltpu.SMEM)
    return pl.pallas_call(
        begin_kernel,
        in_specs=[smem, smem, pl.BlockSpec(memory_space=pl.ANY), vmem],
        out_specs=[vmem, vmem],
        out_shape=[
            jax.ShapeDtypeStruct(slab.shape, BF),
            jax.ShapeDtypeStruct((groups, quantity * tile, occupied), F32),
        ],
        scratch_shapes=[pltpu.SemaphoreType.DMA((groups, quantity))],
        compiler_params=pltpu.CompilerParams(vmem_limit_bytes=VMEM_LIMIT),
        cost_estimate=pl.CostEstimate(
            flops=slab.size * occupied, bytes_accessed=2 * slab.size, transcendentals=0
        ),
    )(parity, screen, slab, orbit)


def half_end(parity, screen, kept, orbit, begun):
    quantity, rows, _ = kept.shape
    vmem = pl.BlockSpec(memory_space=pltpu.VMEM)
    smem = pl.BlockSpec(memory_space=pltpu.SMEM)
    return pl.pallas_call(
        end_kernel,
        in_specs=[smem, smem, vmem, vmem, vmem],
        out_specs=vmem,
        out_shape=jax.ShapeDtypeStruct((rows, quantity * orbit.shape[2]), BF),
        compiler_params=pltpu.CompilerParams(vmem_limit_bytes=VMEM_LIMIT),
        cost_estimate=pl.CostEstimate(
            flops=kept.size * orbit.shape[2], bytes_accessed=kept.size, transcendentals=0
        ),
    )(parity, screen, kept, orbit, begun)


def plain(body, out_shape, scalars, *args):
    vmem = pl.BlockSpec(memory_space=pltpu.VMEM)
    return pl.pallas_call(
        body,
        in_specs=[pl.BlockSpec(memory_space=pltpu.SMEM)] + [vmem] * len(args),
        out_specs=[vmem] * len(out_shape),
        out_shape=out_shape,
        compiler_params=pltpu.CompilerParams(vmem_limit_bytes=VMEM_LIMIT),
        cost_estimate=pl.CostEstimate(
            flops=10**9, bytes_accessed=4 * 10**6, transcendentals=0
        ),
    )(scalars, *args)


def chosen(where_ref, step, rows):
    at = where_ref[step]
    block = rows[0][...]
    for m in (1, 2, 3):
        block = jnp.where(at == m, rows[m][...], block)
    return block


def times(block, cols):
    return lax.dot_general(
        block, cols, (((1,), (1,)), ((), ())), preferred_element_type=F32
    )


def product_kernel(where_ref, r0, r1, r2, r3, c1, c2, c3, c4, *outs):
    n = c1.shape[0]
    for step, out_a, out_b in zip((2, 1, 3, 0), outs[::2], outs[1::2], strict=True):
        block = chosen(where_ref, step, (r0, r1, r2, r3))
        own = times(block, r0[...])
        out_a[:, :n] = times(block, c1[...]).astype(out_a.dtype)
        out_a[:, n : 2 * n] = times(block, c2[...]).astype(out_a.dtype)
        out_a[:, 2 * n :] = own[:, : n // 2].astype(out_a.dtype)
        out_b[:, :n] = times(block, c3[...]).astype(out_b.dtype)
        out_b[:, n : 2 * n] = times(block, c4[...]).astype(out_b.dtype)
        out_b[:, 2 * n :] = own[:, n // 2 :].astype(out_b.dtype)


def relay_kernel(_, up_a, far_a, down_b, far_b, out_a, out_b):
    out_a[...] = (up_a[...] + far_a[...].astype(F32)).astype(BF)
    out_b[...] = (down_b[...] + far_b[...].astype(F32)).astype(BF)


def home_kernel(_, home_a, up_a, down_a, home_b, up_b, down_b, a_ref, b_ref, t1, t2, t3, *, scale):
    n = t1.shape[0]
    a = (home_a[...] + up_a[...].astype(F32) + down_a[...].astype(F32)) * scale
    b = (home_b[...] + up_b[...].astype(F32) + down_b[...].astype(F32)) * scale
    a_ref[...] = a
    b_ref[...] = b
    t1[...] = a[:, :n].astype(BF)
    t2[...] = a[:, n : 2 * n].astype(BF)
    t3[...] = b[:, :n].astype(BF)


def place_kernel(place_ref, a_ref, b_ref, t1, t2, t3, out_ref):
    n = t1.shape[0]

    def at(k):
        return pl.ds(pl.multiple_of(place_ref[k] * n, 128), n)

    out_ref[:, at(1)] = a_ref[:, :n]
    out_ref[:, at(2)] = a_ref[:, n : 2 * n]
    out_ref[:, at(3)] = b_ref[:, :n]
    out_ref[:, at(4)] = b_ref[:, n : 2 * n]
    out_ref[:, at(0)] = jnp.concatenate([a_ref[:, 2 * n :], b_ref[:, 2 * n :]], axis=1)
    out_ref[:, at(7)] = t1[...].astype(F32).T
    out_ref[:, at(6)] = t2[...].astype(F32).T
    out_ref[:, at(5)] = t3[...].astype(F32).T


def on_device(slab, screen, orbitals, hcore):
    quantity, row_count, basis = slab.shape
    occupied = orbitals.shape[1]
    depth = quantity * occupied
    core = lax.axis_index("core")
    aux = lax.axis_index(AUX)
    z = lax.axis_index("z")
    plane = lax.axis_index("y") * 2 + lax.axis_index("xl")
    row_devices = lax.axis_size(ROW)
    scale = 1.0 / math.sqrt(quantity * 4 * occupied)

    own = lax.dynamic_slice_in_dim(orbitals, core * (row_count // 2), row_count // 2, 0)
    mine = lax.all_to_all(
        jnp.broadcast_to(own[None], (row_devices,) + own.shape), ROW, 0, 0, tiled=True
    )
    other = flip(mine, "core", 1, 2)

    kept, begun = half_begin(core[None], screen[0], slab, mine)
    flat = half_end(1 - core[None], screen[0], kept, other, begun)

    swapped = lax.ppermute(
        flat, ("xh", "core", "z"), [(a * 4 + k, k * 4 + a) for a in range(4) for k in range(4)]
    )
    shards = hcore.shape[1] // row_count
    pair = [lax.dynamic_slice_in_dim(v, aux * shards, shards, 0) for v in (mine, other)]
    column_orbitals = jnp.stack(
        [jnp.where(core == 0, *pair), jnp.where(core == 0, *pair[::-1])], axis=1
    ).reshape(hcore.shape[1], occupied)
    high, low = two_term(hcore)
    core_part = jnp.dot(high, column_orbitals, preferred_element_type=F32) + jnp.dot(
        low, column_orbitals, preferred_element_type=F32
    )
    orbit_rows = orbitals.astype(F32)
    core_projection = jnp.dot(orbit_rows.T, core_part, precision=lax.Precision.HIGHEST)
    overlap = lax.dot_general(
        flat, orbitals, (((0,), (0,)), ((), ())), preferred_element_type=F32
    )
    summed = jnp.concatenate([overlap, core_projection], axis=0)

    factors = [swapped, flip(swapped, "core", 1, 2), flip(swapped, "xh", 1, 2)]
    factors.append(flip(factors[2], "core", 1, 2))
    factors += [
        lax.ppermute(swapped, PLANE, [(spot((s + m) % 8), spot(s)) for s in range(8)])
        for m in (1, 2, 3, 4)
    ]
    pieces = summed.reshape(row_devices, -1, occupied)
    piece = jnp.sum(lax.all_to_all(pieces, ROW, 0, 0, tiled=True), axis=0)
    where = ((z + jnp.arange(4, dtype=jnp.int32)) % 4) ^ aux
    part = jax.ShapeDtypeStruct((row_count, 5 * row_count // 2), BF)
    part_f32 = jax.ShapeDtypeStruct(part.shape, F32)
    far_a, far_b, up_a, up_b, down_a, down_b, home_a, home_b = plain(
        product_kernel,
        [part, part, part_f32, part, part, part_f32, part_f32, part_f32],
        where,
        *factors,
    )
    far_a = shift(far_a, "z", 1, 4)
    far_b = shift(far_b, "z", -1, 4)
    up_b = shift(up_b, "z", 1, 4)
    down_a = shift(down_a, "z", -1, 4)
    up_a, down_b = plain(relay_kernel, [part, part], where, up_a, far_a, down_b, far_b)
    up_a = shift(up_a, "z", 1, 4)
    down_b = shift(down_b, "z", -1, 4)
    tile = jax.ShapeDtypeStruct((row_count, row_count), BF)
    home_a, home_b, *tiles = plain(
        functools.partial(home_kernel, scale=scale),
        [part_f32, part_f32, tile, tile, tile],
        where,
        home_a,
        up_a,
        down_a,
        home_b,
        up_b,
        down_b,
    )
    turned = [
        lax.ppermute(
            tile,
            AUX + ROW,
            [
                (a * 32 + k * 8 + spot(s), k * 32 + a * 8 + spot((s + m) % 8))
                for a in range(4)
                for k in range(4)
                for s in range(8)
            ],
        )
        for m, tile in zip((1, 2, 3), tiles, strict=True)
    ]
    place = spot((plane + jnp.arange(8, dtype=jnp.int32)) % 8)
    (exchange,) = plain(
        place_kernel,
        [jax.ShapeDtypeStruct(hcore.shape, F32)],
        place,
        home_a,
        home_b,
        *turned,
    )

    summed = lax.all_to_all(
        jnp.broadcast_to(piece[None], pieces.shape), ROW, 0, 0, tiled=True
    ).reshape(summed.shape)
    overlap, core_projection = summed[:depth], summed[depth:]
    o_high, o_low = two_term(overlap)
    exchange_part = jnp.dot(flat, o_high, preferred_element_type=F32) + jnp.dot(
        flat, o_low, preferred_element_type=F32
    )
    applied = core_part - (0.5 * scale) * exchange_part
    projection = core_projection - (0.5 * scale) * jnp.dot(
        overlap.T, overlap, precision=lax.Precision.HIGHEST
    )
    both = jnp.concatenate([applied, projection], axis=0)
    both = both + flip(both, "core", 1, 2)
    both = both + flip(both, "xh", 1, 2)
    applied, projection = both[:row_count], both[row_count:]
    gradient = applied - jnp.dot(orbit_rows, projection, precision=lax.Precision.HIGHEST)
    return (exchange, gradient)


def solution(mesh):
    finer = Mesh(mesh.devices.reshape(2, 2, 4, 2, 4), AUX + ROW)
    in_specs = (P(AUX, ROW, None), P(AUX, ROW, None), P(ROW, None), P(ROW, AUX))
    out_specs = (P(ROW, AUX), P(ROW, None))
    return jax.shard_map(
        on_device, mesh=finer, in_specs=in_specs, out_specs=out_specs, check_vma=False
    )
```

```python
import functools
import math

import jax
import jax.numpy as jnp
from jax import lax
from jax.experimental import pallas as pl
from jax.experimental.pallas import tpu as pltpu
from jax.sharding import Mesh, PartitionSpec as P

ROW = ("z", "xl", "y")
AUX = ("xh", "core")
PLANE = ("xl", "y")
BF = jnp.bfloat16
F32 = jnp.float32
SHARDS = 8
VMEM_LIMIT = 16 * 1024 * 1024


def flip(value, axis, mask, size):
    return lax.ppermute(value, axis, [(k, k ^ mask) for k in range(size)])


def shift(value, axis, step, size):
    return lax.ppermute(value, axis, [(k, (k + step) % size) for k in range(size)])


def spot(s):
    return (s % 2) * 4 + s // 2


def screened(screen_ref, t, orbit_ref, parity, begin):
    return jnp.concatenate(
        [
            orbit_ref[v] * screen_ref[t, 2 * v + parity].astype(F32).astype(BF)
            for v in range(begin, begin + SHARDS)
        ],
        axis=0,
    )


def one_chunk(parity, screen_ref, slab_ref, orbit_ref, t, begin):
    quantity = slab_ref.shape[0]
    tile = orbit_ref.shape[1]
    block = jnp.concatenate(
        [
            slab_ref[
                :,
                t * tile : (t + 1) * tile,
                pl.ds(pl.multiple_of((2 * v + parity) * tile, tile), tile),
            ].reshape(quantity * tile, tile)
            for v in range(begin, begin + SHARDS)
        ],
        axis=1,
    )
    return jnp.dot(
        block,
        screened(screen_ref, t, orbit_ref, parity, begin),
        preferred_element_type=F32,
    )


def begin_kernel(parity_ref, screen_ref, slab_ref, orbit_ref, kept_ref, out_ref, sems):
    quantity, rows, _ = kept_ref.shape
    shards, tile, _ = orbit_ref.shape
    groups = rows // tile
    width = 2 * SHARDS * tile
    chunks = shards // SHARDS
    copies = [
        pltpu.make_async_copy(
            slab_ref.at[:, :, pl.ds(c * width, width)],
            kept_ref.at[:, :, pl.ds(c * width, width)],
            sems.at[c],
        )
        for c in range(chunks)
    ]
    copies[0].start()
    copies[1].start()
    for c in range(chunks):
        copies[c].wait()
        if c + 2 < chunks:
            copies[c + 2].start()
        for t in range(groups):
            term = one_chunk(
                parity_ref[0], screen_ref, kept_ref, orbit_ref, t, c * SHARDS
            )
            out_ref[t] = term if c == 0 else out_ref[t] + term


def end_kernel(parity_ref, screen_ref, kept_ref, orbit_ref, begun_ref, out_ref):
    quantity, rows, _ = kept_ref.shape
    tile = orbit_ref.shape[1]
    for t in range(rows // tile):
        total = begun_ref[t]
        for begin in range(0, orbit_ref.shape[0], SHARDS):
            total = total + one_chunk(
                parity_ref[0], screen_ref, kept_ref, orbit_ref, t, begin
            )
        for q in range(quantity):
            out_ref[t * tile : (t + 1) * tile, q * tile : (q + 1) * tile] = total[
                q * tile : (q + 1) * tile
            ].astype(BF)


def half_begin(parity, screen, slab, orbit):
    quantity, rows, _ = slab.shape
    _, tile, occupied = orbit.shape
    groups = rows // tile
    vmem = pl.BlockSpec(memory_space=pltpu.VMEM)
    smem = pl.BlockSpec(memory_space=pltpu.SMEM)
    return pl.pallas_call(
        begin_kernel,
        in_specs=[smem, smem, pl.BlockSpec(memory_space=pl.ANY), vmem],
        out_specs=[vmem, vmem],
        out_shape=[
            jax.ShapeDtypeStruct(slab.shape, BF),
            jax.ShapeDtypeStruct((groups, quantity * tile, occupied), F32),
        ],
        scratch_shapes=[pltpu.SemaphoreType.DMA((orbit.shape[0] // SHARDS,))],
        compiler_params=pltpu.CompilerParams(vmem_limit_bytes=VMEM_LIMIT),
        cost_estimate=pl.CostEstimate(
            flops=slab.size * occupied, bytes_accessed=2 * slab.size, transcendentals=0
        ),
    )(parity, screen, slab, orbit)


def half_end(parity, screen, kept, orbit, begun):
    quantity, rows, _ = kept.shape
    vmem = pl.BlockSpec(memory_space=pltpu.VMEM)
    smem = pl.BlockSpec(memory_space=pltpu.SMEM)
    return pl.pallas_call(
        end_kernel,
        in_specs=[smem, smem, vmem, vmem, vmem],
        out_specs=vmem,
        out_shape=jax.ShapeDtypeStruct((rows, quantity * orbit.shape[2]), BF),
        compiler_params=pltpu.CompilerParams(vmem_limit_bytes=VMEM_LIMIT),
        cost_estimate=pl.CostEstimate(
            flops=kept.size * orbit.shape[2], bytes_accessed=kept.size, transcendentals=0
        ),
    )(parity, screen, kept, orbit, begun)


def plain(body, out_shape, scalars, *args, flops=10**9, limit=8 * 1024 * 1024):
    vmem = pl.BlockSpec(memory_space=pltpu.VMEM)
    return pl.pallas_call(
        body,
        in_specs=[pl.BlockSpec(memory_space=pltpu.SMEM)] + [vmem] * len(args),
        out_specs=[vmem] * len(out_shape),
        out_shape=out_shape,
        compiler_params=pltpu.CompilerParams(vmem_limit_bytes=limit),
        cost_estimate=pl.CostEstimate(
            flops=flops, bytes_accessed=4 * 10**6, transcendentals=0
        ),
    )(scalars, *args)


def chosen(where_ref, step, rows):
    at = where_ref[step]
    block = rows[0][...]
    for m in (1, 2, 3):
        block = jnp.where(at == m, rows[m][...], block)
    return block


def times(block, cols):
    return lax.dot_general(
        block, cols, (((1,), (1,)), ((), ())), preferred_element_type=F32
    )


def product_kernel(where_ref, r0, r1, r2, r3, c1, c2, c3, c4, *outs):
    n = c1.shape[0]
    for step, out_a, out_b in zip((2, 1, 3, 0), outs[::2], outs[1::2], strict=True):
        block = chosen(where_ref, step, (r0, r1, r2, r3))
        own = times(block, r0[...])
        out_a[:, :n] = times(block, c1[...]).astype(out_a.dtype)
        out_a[:, n : 2 * n] = times(block, c2[...]).astype(out_a.dtype)
        out_a[:, 2 * n :] = own[:, : n // 2].astype(out_a.dtype)
        out_b[:, :n] = times(block, c3[...]).astype(out_b.dtype)
        out_b[:, n : 2 * n] = times(block, c4[...]).astype(out_b.dtype)
        out_b[:, 2 * n :] = own[:, n // 2 :].astype(out_b.dtype)


def relay_kernel(_, up_a, far_a, down_b, far_b, out_a, out_b):
    out_a[...] = (up_a[...] + far_a[...].astype(F32)).astype(BF)
    out_b[...] = (down_b[...] + far_b[...].astype(F32)).astype(BF)


def home_kernel(
    place_ref, home_a, up_a, down_a, home_b, up_b, down_b, out_ref, t1, t2, t3, *, scale
):
    n = t1.shape[0]

    def at(k):
        return pl.ds(pl.multiple_of(place_ref[k] * n, 128), n)

    a = (home_a[...] + up_a[...].astype(F32) + down_a[...].astype(F32)) * scale
    b = (home_b[...] + up_b[...].astype(F32) + down_b[...].astype(F32)) * scale
    t1[...] = a[:, :n].astype(BF)
    t2[...] = a[:, n : 2 * n].astype(BF)
    t3[...] = b[:, :n].astype(BF)
    out_ref[:, at(1)] = a[:, :n]
    out_ref[:, at(2)] = a[:, n : 2 * n]
    out_ref[:, at(3)] = b[:, :n]
    out_ref[:, at(4)] = b[:, n : 2 * n]
    out_ref[:, at(0)] = jnp.concatenate([a[:, 2 * n :], b[:, 2 * n :]], axis=1)


def two_terms(value):
    high = value.astype(BF)
    return high, (value - high.astype(F32)).astype(BF)


def inner(left, right):
    return lax.dot_general(left, right, (((0,), (0,)), ((), ())), preferred_element_type=F32)


def outer(left, right):
    return jnp.dot(left, right, preferred_element_type=F32)


def sums_kernel(where_ref, flat_ref, orbit_ref, mine_ref, other_ref, hcore_ref, out_ref, part_ref):
    depth = flat_ref.shape[1]
    tile = mine_ref.shape[1]
    shards = hcore_ref.shape[1] // (2 * tile)
    begins_here = where_ref[0] == 0
    columns = []
    for v in range(shards):
        at = where_ref[1] * shards + v
        mine, other = mine_ref[at], other_ref[at]
        columns.append(jnp.where(begins_here, mine, other))
        columns.append(jnp.where(begins_here, other, mine))
    columns = jnp.concatenate(columns, axis=0)
    high, low = two_terms(hcore_ref[...])
    part = outer(high, columns) + outer(low, columns)
    part_ref[...] = part
    orbit = orbit_ref[...]
    high, low = two_terms(part)
    out_ref[:depth] = inner(flat_ref[...], orbit)
    out_ref[depth:] = inner(orbit, high) + inner(orbit, low)


def spread_kernel(_, pieces_ref, out_ref):
    total = jnp.sum(pieces_ref[...], axis=0)
    out_ref[...] = jnp.broadcast_to(total[None], out_ref.shape)


def applied_kernel(_, flat_ref, summed_ref, part_ref, out_ref, *, factor):
    rows, depth = flat_ref.shape
    high, low = two_terms(summed_ref[:depth])
    flat = flat_ref[...]
    out_ref[:rows] = part_ref[...] - factor * (outer(flat, high) + outer(flat, low))
    out_ref[rows:] = summed_ref[depth:] - factor * (
        inner(high, high) + inner(high, low) + inner(low, high)
    )


def add_kernel(_, left, right, out_ref):
    out_ref[...] = left[...] + right[...]


def gradient_kernel(_, orbit_ref, left, right, out_ref):
    rows = orbit_ref.shape[0]
    high, low = two_terms(left[rows:] + right[rows:])
    orbit = orbit_ref[...]
    out_ref[...] = left[:rows] + right[:rows] - (outer(orbit, high) + outer(orbit, low))


def place_kernel(place_ref, t1, t2, t3, _, out_ref, turned, sems):
    n = t1.shape[0]
    copies = []
    for k, tile in enumerate((t1, t2, t3)):
        turned[k] = tile[...].astype(F32).T
        at = pl.ds(pl.multiple_of(place_ref[7 - k] * n, 128), n)
        copies.append(pltpu.make_async_copy(turned.at[k], out_ref.at[:, at], sems.at[k]))
        copies[-1].start()
    for copy in copies:
        copy.wait()


def place(where, tiles, out):
    n = tiles[0].shape[0]
    vmem = pl.BlockSpec(memory_space=pltpu.VMEM)
    hbm = pl.BlockSpec(memory_space=pl.ANY)
    return pl.pallas_call(
        place_kernel,
        in_specs=[pl.BlockSpec(memory_space=pltpu.SMEM)] + [vmem] * 3 + [hbm],
        out_specs=hbm,
        out_shape=jax.ShapeDtypeStruct(out.shape, out.dtype),
        input_output_aliases={4: 0},
        scratch_shapes=[pltpu.VMEM((3, n, n), F32), pltpu.SemaphoreType.DMA((3,))],
        compiler_params=pltpu.CompilerParams(vmem_limit_bytes=VMEM_LIMIT),
    )(where, *tiles, out)


def on_device(slab, screen, orbitals, hcore):
    quantity, row_count, basis = slab.shape
    occupied = orbitals.shape[1]
    depth = quantity * occupied
    core = lax.axis_index("core")
    aux = lax.axis_index(AUX)
    z = lax.axis_index("z")
    plane = lax.axis_index("y") * 2 + lax.axis_index("xl")
    row_devices = lax.axis_size(ROW)
    scale = 1.0 / math.sqrt(quantity * 4 * occupied)

    own = lax.dynamic_slice_in_dim(orbitals, core * (row_count // 2), row_count // 2, 0)
    where = ((z + jnp.arange(4, dtype=jnp.int32)) % 4) ^ aux
    spots = spot((plane + jnp.arange(8, dtype=jnp.int32)) % 8)
    own, here, there, ids, where, spots = lax.optimization_barrier(
        (own, core[None], 1 - core[None], jnp.stack([core, aux]), where, spots)
    )
    mine = lax.all_to_all(
        jnp.broadcast_to(own[None], (row_devices,) + own.shape), ROW, 0, 0, tiled=True
    )
    other = flip(mine, "core", 1, 2)

    kept, begun = half_begin(here, screen[0], slab, mine)
    flat = half_end(there, screen[0], kept, other, begun)

    swapped = lax.ppermute(
        flat, ("xh", "core", "z"), [(a * 4 + k, k * 4 + a) for a in range(4) for k in range(4)]
    )
    summed, core_part = plain(
        sums_kernel,
        [
            jax.ShapeDtypeStruct((depth + occupied, occupied), F32),
            jax.ShapeDtypeStruct((row_count, occupied), F32),
        ],
        ids,
        flat,
        orbitals,
        mine,
        other,
        hcore,
        flops=10**10,
    )

    far_rows = flip(swapped, "xh", 1, 2)
    columns = [
        lax.ppermute(swapped, PLANE, [(spot((s + m) % 8), spot(s)) for s in range(8)])
        for m in (1, 2, 3, 4)
    ]
    swapped, far_rows = lax.optimization_barrier((swapped, far_rows))
    factors = [swapped, flip(swapped, "core", 1, 2), far_rows, flip(far_rows, "core", 1, 2)]
    factors += columns
    pieces = summed.reshape(row_devices, -1, occupied)
    pieces = lax.all_to_all(pieces, ROW, 0, 0, tiled=True)
    pieces, factors[4] = lax.optimization_barrier((pieces, factors[4]))
    part = jax.ShapeDtypeStruct((row_count, 5 * row_count // 2), BF)
    part_f32 = jax.ShapeDtypeStruct(part.shape, F32)
    far_a, far_b, up_a, up_b, down_a, down_b, home_a, home_b = plain(
        product_kernel,
        [part, part, part_f32, part, part, part_f32, part_f32, part_f32],
        where,
        *factors,
    )
    (pieces,) = plain(
        spread_kernel,
        [jax.ShapeDtypeStruct(pieces.shape, F32)],
        where,
        pieces,
        flops=10**10,
    )
    far_a = shift(far_a, "z", 1, 4)
    far_b = shift(far_b, "z", -1, 4)
    up_b = shift(up_b, "z", 1, 4)
    down_a = shift(down_a, "z", -1, 4)
    up_a, down_b = plain(relay_kernel, [part, part], where, up_a, far_a, down_b, far_b)
    up_a = shift(up_a, "z", 1, 4)
    down_b = shift(down_b, "z", -1, 4)
    tile = jax.ShapeDtypeStruct((row_count, row_count), BF)
    exchange, *tiles = plain(
        functools.partial(home_kernel, scale=scale),
        [jax.ShapeDtypeStruct(hcore.shape, F32), tile, tile, tile],
        spots,
        home_a,
        up_a,
        down_a,
        home_b,
        up_b,
        down_b,
    )
    turned = [
        lax.ppermute(
            tile,
            AUX + ROW,
            [
                (a * 32 + k * 8 + spot(s), k * 32 + a * 8 + spot((s + m) % 8))
                for a in range(4)
                for k in range(4)
                for s in range(8)
            ],
        )
        for m, tile in zip((1, 2, 3), tiles, strict=True)
    ]
    exchange = place(spots, turned, exchange)

    summed = lax.all_to_all(pieces, ROW, 0, 0, tiled=True).reshape(summed.shape)
    (both,) = plain(
        functools.partial(applied_kernel, factor=0.5 * scale),
        [jax.ShapeDtypeStruct((row_count + occupied, occupied), F32)],
        where,
        flat,
        summed,
        core_part,
    )
    (both,) = plain(
        add_kernel,
        [jax.ShapeDtypeStruct(both.shape, F32)],
        where,
        both,
        flip(both, "core", 1, 2),
    )
    (gradient,) = plain(
        gradient_kernel,
        [jax.ShapeDtypeStruct((row_count, occupied), F32)],
        where,
        orbitals,
        both,
        flip(both, "xh", 1, 2),
    )
    return (exchange, gradient)


def solution(mesh):
    finer = Mesh(mesh.devices.reshape(2, 2, 4, 2, 4), AUX + ROW)
    in_specs = (P(AUX, ROW, None), P(AUX, ROW, None), P(ROW, None), P(ROW, AUX))
    out_specs = (P(ROW, AUX), P(ROW, None))
    return jax.shard_map(
        on_device, mesh=finer, in_specs=in_specs, out_specs=out_specs, check_vma=False
    )
```

```python
import functools
import math

import jax
import jax.numpy as jnp
from jax import lax
from jax.experimental import pallas as pl
from jax.experimental.pallas import tpu as pltpu
from jax.sharding import Mesh, PartitionSpec as P

ROW = ("z", "xl", "y")
AUX = ("xh", "core")
PLANE = ("xl", "y")
BF = jnp.bfloat16
F32 = jnp.float32
SHARDS = 8
OFFSETS = (1, 6, 3, 4)
VMEM_LIMIT = 16 * 1024 * 1024


def flip(value, axis, mask, size):
    return lax.ppermute(value, axis, [(k, k ^ mask) for k in range(size)])


def shift(value, axis, step, size):
    return lax.ppermute(value, axis, [(k, (k + step) % size) for k in range(size)])


def spot(s):
    return (s % 2) * 4 + s // 2


def screened(screen_ref, t, orbit_ref, parity, begin):
    return jnp.concatenate(
        [
            orbit_ref[v] * screen_ref[t, 2 * v + parity].astype(F32).astype(BF)
            for v in range(begin, begin + SHARDS)
        ],
        axis=0,
    )


def one_chunk(parity, screen_ref, slab_ref, orbit_ref, t, begin):
    quantity = slab_ref.shape[0]
    tile = orbit_ref.shape[1]
    block = jnp.concatenate(
        [
            slab_ref[
                :,
                t * tile : (t + 1) * tile,
                pl.ds(pl.multiple_of((2 * v + parity) * tile, tile), tile),
            ].reshape(quantity * tile, tile)
            for v in range(begin, begin + SHARDS)
        ],
        axis=1,
    )
    return jnp.dot(
        block,
        screened(screen_ref, t, orbit_ref, parity, begin),
        preferred_element_type=F32,
    )


def begin_kernel(parity_ref, screen_ref, slab_ref, orbit_ref, kept_ref, out_ref, sems):
    quantity, rows, _ = kept_ref.shape
    shards, tile, _ = orbit_ref.shape
    groups = rows // tile
    width = 2 * SHARDS * tile
    chunks = shards // SHARDS
    copies = [
        pltpu.make_async_copy(
            slab_ref.at[:, :, pl.ds(c * width, width)],
            kept_ref.at[:, :, pl.ds(c * width, width)],
            sems.at[c],
        )
        for c in range(chunks)
    ]
    copies[0].start()
    copies[1].start()
    for c in range(chunks):
        copies[c].wait()
        if c + 2 < chunks:
            copies[c + 2].start()
        for t in range(groups):
            term = one_chunk(
                parity_ref[0], screen_ref, kept_ref, orbit_ref, t, c * SHARDS
            )
            out_ref[t] = term if c == 0 else out_ref[t] + term


def end_kernel(parity_ref, screen_ref, kept_ref, orbit_ref, begun_ref, out_ref):
    quantity, rows, _ = kept_ref.shape
    tile = orbit_ref.shape[1]
    for t in range(rows // tile):
        total = begun_ref[t]
        for begin in range(0, orbit_ref.shape[0], SHARDS):
            total = total + one_chunk(
                parity_ref[0], screen_ref, kept_ref, orbit_ref, t, begin
            )
        for q in range(quantity):
            out_ref[t * tile : (t + 1) * tile, q * tile : (q + 1) * tile] = total[
                q * tile : (q + 1) * tile
            ].astype(BF)


def half_begin(parity, screen, slab, orbit):
    quantity, rows, _ = slab.shape
    _, tile, occupied = orbit.shape
    groups = rows // tile
    vmem = pl.BlockSpec(memory_space=pltpu.VMEM)
    smem = pl.BlockSpec(memory_space=pltpu.SMEM)
    return pl.pallas_call(
        begin_kernel,
        in_specs=[smem, smem, pl.BlockSpec(memory_space=pl.ANY), vmem],
        out_specs=[vmem, vmem],
        out_shape=[
            jax.ShapeDtypeStruct(slab.shape, BF),
            jax.ShapeDtypeStruct((groups, quantity * tile, occupied), F32),
        ],
        scratch_shapes=[pltpu.SemaphoreType.DMA((orbit.shape[0] // SHARDS,))],
        compiler_params=pltpu.CompilerParams(vmem_limit_bytes=VMEM_LIMIT),
        cost_estimate=pl.CostEstimate(
            flops=slab.size * occupied, bytes_accessed=2 * slab.size, transcendentals=0
        ),
    )(parity, screen, slab, orbit)


def half_end(parity, screen, kept, orbit, begun):
    quantity, rows, _ = kept.shape
    vmem = pl.BlockSpec(memory_space=pltpu.VMEM)
    smem = pl.BlockSpec(memory_space=pltpu.SMEM)
    return pl.pallas_call(
        end_kernel,
        in_specs=[smem, smem, vmem, vmem, vmem],
        out_specs=vmem,
        out_shape=jax.ShapeDtypeStruct((rows, quantity * orbit.shape[2]), BF),
        compiler_params=pltpu.CompilerParams(vmem_limit_bytes=VMEM_LIMIT),
        cost_estimate=pl.CostEstimate(
            flops=kept.size * orbit.shape[2], bytes_accessed=kept.size, transcendentals=0
        ),
    )(parity, screen, kept, orbit, begun)


def plain(body, out_shape, scalars, *args, flops=10**9, limit=8 * 1024 * 1024):
    vmem = pl.BlockSpec(memory_space=pltpu.VMEM)
    return pl.pallas_call(
        body,
        in_specs=[pl.BlockSpec(memory_space=pltpu.SMEM)] + [vmem] * len(args),
        out_specs=[vmem] * len(out_shape),
        out_shape=out_shape,
        compiler_params=pltpu.CompilerParams(vmem_limit_bytes=limit),
        cost_estimate=pl.CostEstimate(
            flops=flops, bytes_accessed=4 * 10**6, transcendentals=0
        ),
    )(scalars, *args)


def chosen(where_ref, step, rows):
    at = where_ref[step]
    block = rows[0][...]
    for m in (1, 2, 3):
        block = jnp.where(at == m, rows[m][...], block)
    return block


def times(block, cols):
    return lax.dot_general(
        block, cols, (((1,), (1,)), ((), ())), preferred_element_type=F32
    )


def product_kernel(where_ref, r0, r1, r2, r3, c1, c2, c3, c4, *outs):
    n = c1.shape[0]
    for step, out_a, out_b in zip((2, 1, 3, 0), outs[::2], outs[1::2], strict=True):
        block = chosen(where_ref, step, (r0, r1, r2, r3))
        own = times(block, r0[...])
        out_a[:, :n] = times(block, c1[...]).astype(out_a.dtype)
        out_a[:, n : 2 * n] = times(block, c2[...]).astype(out_a.dtype)
        out_a[:, 2 * n :] = own[:, : n // 2].astype(out_a.dtype)
        out_b[:, :n] = times(block, c3[...]).astype(out_b.dtype)
        out_b[:, n : 2 * n] = times(block, c4[...]).astype(out_b.dtype)
        out_b[:, 2 * n :] = own[:, n // 2 :].astype(out_b.dtype)


def relay_kernel(_, up_a, far_a, down_b, far_b, out_a, out_b):
    out_a[...] = (up_a[...] + far_a[...].astype(F32)).astype(BF)
    out_b[...] = (down_b[...] + far_b[...].astype(F32)).astype(BF)


def home_kernel(
    place_ref, home_a, up_a, down_a, home_b, up_b, down_b, out_ref, t1, t2, t3, *, scale
):
    n = t1.shape[0]

    def at(k):
        return pl.ds(pl.multiple_of(place_ref[k] * n, 128), n)

    a = (home_a[...] + up_a[...].astype(F32) + down_a[...].astype(F32)) * scale
    b = (home_b[...] + up_b[...].astype(F32) + down_b[...].astype(F32)) * scale
    t1[...] = a[:, :n].astype(BF)
    t2[...] = a[:, n : 2 * n].astype(BF)
    t3[...] = b[:, :n].astype(BF)
    out_ref[:, at(1)] = a[:, :n]
    out_ref[:, at(6)] = a[:, n : 2 * n]
    out_ref[:, at(3)] = b[:, :n]
    out_ref[:, at(4)] = b[:, n : 2 * n]
    out_ref[:, at(0)] = jnp.concatenate([a[:, 2 * n :], b[:, 2 * n :]], axis=1)


def two_terms(value):
    high = value.astype(BF)
    return high, (value - high.astype(F32)).astype(BF)


def inner(left, right):
    return lax.dot_general(left, right, (((0,), (0,)), ((), ())), preferred_element_type=F32)


def outer(left, right):
    return jnp.dot(left, right, preferred_element_type=F32)


def sums_kernel(where_ref, flat_ref, orbit_ref, mine_ref, other_ref, hcore_ref, out_ref, part_ref):
    depth = flat_ref.shape[1]
    tile = mine_ref.shape[1]
    shards = hcore_ref.shape[1] // (2 * tile)
    begins_here = where_ref[0] == 0
    columns = []
    for v in range(shards):
        at = where_ref[1] * shards + v
        mine, other = mine_ref[at], other_ref[at]
        columns.append(jnp.where(begins_here, mine, other))
        columns.append(jnp.where(begins_here, other, mine))
    columns = jnp.concatenate(columns, axis=0)
    high, low = two_terms(hcore_ref[...])
    part = outer(high, columns) + outer(low, columns)
    part_ref[...] = part
    orbit = orbit_ref[...]
    high, low = two_terms(part)
    out_ref[:depth] = inner(flat_ref[...], orbit)
    out_ref[depth:] = inner(orbit, high) + inner(orbit, low)


def spread_kernel(_, pieces_ref, out_ref):
    total = jnp.sum(pieces_ref[...], axis=0)
    out_ref[...] = jnp.broadcast_to(total[None], out_ref.shape)


def applied_kernel(_, flat_ref, summed_ref, part_ref, out_ref, *, factor):
    rows, depth = flat_ref.shape
    high, low = two_terms(summed_ref[:depth])
    flat = flat_ref[...]
    out_ref[:rows] = part_ref[...] - factor * (outer(flat, high) + outer(flat, low))
    out_ref[rows:] = summed_ref[depth:] - factor * (
        inner(high, high) + inner(high, low) + inner(low, high)
    )


def add_kernel(_, left, right, out_ref):
    out_ref[...] = left[...] + right[...]


def gradient_kernel(_, orbit_ref, left, right, out_ref):
    rows = orbit_ref.shape[0]
    high, low = two_terms(left[rows:] + right[rows:])
    orbit = orbit_ref[...]
    out_ref[...] = left[:rows] + right[:rows] - (outer(orbit, high) + outer(orbit, low))


def place_kernel(place_ref, t1, t2, t3, _, out_ref, turned, sems):
    n = t1.shape[0]
    copies = []
    for k, tile in enumerate((t1, t2, t3)):
        turned[k] = tile[...].astype(F32).T
        at = pl.ds(pl.multiple_of(place_ref[8 - OFFSETS[k]] * n, 128), n)
        copies.append(pltpu.make_async_copy(turned.at[k], out_ref.at[:, at], sems.at[k]))
        copies[-1].start()
    for copy in copies:
        copy.wait()


def place(where, tiles, out):
    n = tiles[0].shape[0]
    vmem = pl.BlockSpec(memory_space=pltpu.VMEM)
    hbm = pl.BlockSpec(memory_space=pl.ANY)
    return pl.pallas_call(
        place_kernel,
        in_specs=[pl.BlockSpec(memory_space=pltpu.SMEM)] + [vmem] * 3 + [hbm],
        out_specs=hbm,
        out_shape=jax.ShapeDtypeStruct(out.shape, out.dtype),
        input_output_aliases={4: 0},
        scratch_shapes=[pltpu.VMEM((3, n, n), F32), pltpu.SemaphoreType.DMA((3,))],
        compiler_params=pltpu.CompilerParams(vmem_limit_bytes=VMEM_LIMIT),
    )(where, *tiles, out)


def on_device(slab, screen, orbitals, hcore):
    quantity, row_count, basis = slab.shape
    occupied = orbitals.shape[1]
    depth = quantity * occupied
    core = lax.axis_index("core")
    aux = lax.axis_index(AUX)
    z = lax.axis_index("z")
    plane = lax.axis_index("y") * 2 + lax.axis_index("xl")
    row_devices = lax.axis_size(ROW)
    scale = 1.0 / math.sqrt(quantity * 4 * occupied)

    own = lax.dynamic_slice_in_dim(orbitals, core * (row_count // 2), row_count // 2, 0)
    where = ((z + jnp.arange(4, dtype=jnp.int32)) % 4) ^ aux
    spots = spot((plane + jnp.arange(8, dtype=jnp.int32)) % 8)
    own, here, there, ids, where, spots = lax.optimization_barrier(
        (own, core[None], 1 - core[None], jnp.stack([core, aux]), where, spots)
    )
    mine = lax.all_to_all(
        jnp.broadcast_to(own[None], (row_devices,) + own.shape), ROW, 0, 0, tiled=True
    )
    other = flip(mine, "core", 1, 2)

    kept, begun = half_begin(here, screen[0], slab, mine)
    flat = half_end(there, screen[0], kept, other, begun)

    swapped, far_rows = [
        lax.ppermute(
            flat,
            ("xh", "core", "z"),
            [(a * 4 + k, (k ^ m) * 4 + a) for a in range(4) for k in range(4)],
        )
        for m in (0, 2)
    ]
    swapped, far_rows = lax.optimization_barrier((swapped, far_rows))
    summed, core_part = plain(
        sums_kernel,
        [
            jax.ShapeDtypeStruct((depth + occupied, occupied), F32),
            jax.ShapeDtypeStruct((row_count, occupied), F32),
        ],
        ids,
        flat,
        orbitals,
        mine,
        other,
        hcore,
        flops=10**10,
    )

    columns = [
        lax.ppermute(swapped, PLANE, [(spot((s + m) % 8), spot(s)) for s in range(8)])
        for m in OFFSETS
    ]
    factors = [swapped, flip(swapped, "core", 1, 2), far_rows, flip(far_rows, "core", 1, 2)]
    factors += columns
    pieces = summed.reshape(row_devices, -1, occupied)
    pieces = lax.all_to_all(pieces, ROW, 0, 0, tiled=True)
    pieces, factors[4] = lax.optimization_barrier((pieces, factors[4]))
    part = jax.ShapeDtypeStruct((row_count, 5 * row_count // 2), BF)
    part_f32 = jax.ShapeDtypeStruct(part.shape, F32)
    far_a, far_b, up_a, up_b, down_a, down_b, home_a, home_b = plain(
        product_kernel,
        [part, part, part_f32, part, part, part_f32, part_f32, part_f32],
        where,
        *factors,
    )
    (pieces,) = plain(
        spread_kernel,
        [jax.ShapeDtypeStruct(pieces.shape, F32)],
        where,
        pieces,
        flops=10**10,
    )
    far_a = shift(far_a, "z", 1, 4)
    far_b = shift(far_b, "z", -1, 4)
    up_b = shift(up_b, "z", 1, 4)
    down_a = shift(down_a, "z", -1, 4)
    up_a, down_b = plain(relay_kernel, [part, part], where, up_a, far_a, down_b, far_b)
    up_a = shift(up_a, "z", 1, 4)
    down_b = shift(down_b, "z", -1, 4)
    tile = jax.ShapeDtypeStruct((row_count, row_count), BF)
    exchange, *tiles = plain(
        functools.partial(home_kernel, scale=scale),
        [jax.ShapeDtypeStruct(hcore.shape, F32), tile, tile, tile],
        spots,
        home_a,
        up_a,
        down_a,
        home_b,
        up_b,
        down_b,
    )
    turned = [
        lax.ppermute(
            tile,
            AUX + ROW,
            [
                (a * 32 + k * 8 + spot(s), k * 32 + a * 8 + spot((s + m) % 8))
                for a in range(4)
                for k in range(4)
                for s in range(8)
            ],
        )
        for m, tile in zip(OFFSETS, tiles, strict=False)
    ]
    exchange = place(spots, turned, exchange)

    summed = lax.all_to_all(pieces, ROW, 0, 0, tiled=True).reshape(summed.shape)
    (both,) = plain(
        functools.partial(applied_kernel, factor=0.5 * scale),
        [jax.ShapeDtypeStruct((row_count + occupied, occupied), F32)],
        where,
        flat,
        summed,
        core_part,
    )
    (both,) = plain(
        add_kernel,
        [jax.ShapeDtypeStruct(both.shape, F32)],
        where,
        both,
        flip(both, "core", 1, 2),
    )
    (gradient,) = plain(
        gradient_kernel,
        [jax.ShapeDtypeStruct((row_count, occupied), F32)],
        where,
        orbitals,
        both,
        flip(both, "xh", 1, 2),
    )
    return (exchange, gradient)


def solution(mesh):
    finer = Mesh(mesh.devices.reshape(2, 2, 4, 2, 4), AUX + ROW)
    in_specs = (P(AUX, ROW, None), P(AUX, ROW, None), P(ROW, None), P(ROW, AUX))
    out_specs = (P(ROW, AUX), P(ROW, None))
    return jax.shard_map(
        on_device, mesh=finer, in_specs=in_specs, out_specs=out_specs, check_vma=False
    )
```

```python
import functools
import math

import jax
import jax.numpy as jnp
from jax import lax
from jax.experimental import pallas as pl
from jax.experimental.pallas import tpu as pltpu
from jax.sharding import Mesh, PartitionSpec as P

ROW = ("z", "xl", "y")
AUX = ("xh", "core")
PLANE = ("xl", "y")
BF = jnp.bfloat16
F32 = jnp.float32
SHARDS = 8
OFFSETS = (1, 6, 3, 4)
VMEM_LIMIT = 16 * 1024 * 1024


def flip(value, axis, mask, size):
    return lax.ppermute(value, axis, [(k, k ^ mask) for k in range(size)])


def shift(value, axis, step, size):
    return lax.ppermute(value, axis, [(k, (k + step) % size) for k in range(size)])


def spot(s):
    return (s % 2) * 4 + s // 2


def screened(screen_ref, t, orbit_ref, parity, begin):
    return jnp.concatenate(
        [
            orbit_ref[v] * screen_ref[t, 2 * v + parity].astype(F32).astype(BF)
            for v in range(begin, begin + SHARDS)
        ],
        axis=0,
    )


def one_chunk(parity, screen_ref, slab_ref, orbit_ref, t, begin):
    quantity = slab_ref.shape[0]
    tile = orbit_ref.shape[1]
    block = jnp.concatenate(
        [
            slab_ref[
                :,
                t * tile : (t + 1) * tile,
                pl.ds(pl.multiple_of((2 * v + parity) * tile, tile), tile),
            ].reshape(quantity * tile, tile)
            for v in range(begin, begin + SHARDS)
        ],
        axis=1,
    )
    return jnp.dot(
        block,
        screened(screen_ref, t, orbit_ref, parity, begin),
        preferred_element_type=F32,
    )


def begin_kernel(parity_ref, screen_ref, slab_ref, orbit_ref, kept_ref, out_ref, sems):
    quantity, rows, _ = kept_ref.shape
    shards, tile, _ = orbit_ref.shape
    groups = rows // tile
    width = 2 * SHARDS * tile
    chunks = shards // SHARDS
    copies = [
        pltpu.make_async_copy(
            slab_ref.at[:, :, pl.ds(c * width, width)],
            kept_ref.at[:, :, pl.ds(c * width, width)],
            sems.at[c],
        )
        for c in range(chunks)
    ]
    copies[0].start()
    copies[1].start()
    for c in range(chunks):
        copies[c].wait()
        if c + 2 < chunks:
            copies[c + 2].start()
        for t in range(groups):
            term = one_chunk(
                parity_ref[0], screen_ref, kept_ref, orbit_ref, t, c * SHARDS
            )
            out_ref[t] = term if c == 0 else out_ref[t] + term


def end_kernel(parity_ref, screen_ref, kept_ref, orbit_ref, begun_ref, out_ref):
    quantity, rows, _ = kept_ref.shape
    tile = orbit_ref.shape[1]
    for t in range(rows // tile):
        total = begun_ref[t]
        for begin in range(0, orbit_ref.shape[0], SHARDS):
            total = total + one_chunk(
                parity_ref[0], screen_ref, kept_ref, orbit_ref, t, begin
            )
        for q in range(quantity):
            out_ref[t * tile : (t + 1) * tile, q * tile : (q + 1) * tile] = total[
                q * tile : (q + 1) * tile
            ].astype(BF)


def half_begin(parity, screen, slab, orbit):
    quantity, rows, _ = slab.shape
    _, tile, occupied = orbit.shape
    groups = rows // tile
    vmem = pl.BlockSpec(memory_space=pltpu.VMEM)
    smem = pl.BlockSpec(memory_space=pltpu.SMEM)
    return pl.pallas_call(
        begin_kernel,
        in_specs=[smem, smem, pl.BlockSpec(memory_space=pl.ANY), vmem],
        out_specs=[vmem, vmem],
        out_shape=[
            jax.ShapeDtypeStruct(slab.shape, BF),
            jax.ShapeDtypeStruct((groups, quantity * tile, occupied), F32),
        ],
        scratch_shapes=[pltpu.SemaphoreType.DMA((orbit.shape[0] // SHARDS,))],
        compiler_params=pltpu.CompilerParams(vmem_limit_bytes=VMEM_LIMIT),
        cost_estimate=pl.CostEstimate(
            flops=slab.size * occupied, bytes_accessed=2 * slab.size, transcendentals=0
        ),
    )(parity, screen, slab, orbit)


def half_end(parity, screen, kept, orbit, begun):
    quantity, rows, _ = kept.shape
    vmem = pl.BlockSpec(memory_space=pltpu.VMEM)
    smem = pl.BlockSpec(memory_space=pltpu.SMEM)
    return pl.pallas_call(
        end_kernel,
        in_specs=[smem, smem, vmem, vmem, vmem],
        out_specs=vmem,
        out_shape=jax.ShapeDtypeStruct((rows, quantity * orbit.shape[2]), BF),
        compiler_params=pltpu.CompilerParams(vmem_limit_bytes=VMEM_LIMIT),
        cost_estimate=pl.CostEstimate(
            flops=kept.size * orbit.shape[2], bytes_accessed=kept.size, transcendentals=0
        ),
    )(parity, screen, kept, orbit, begun)


def plain(body, out_shape, scalars, *args, flops=10**9, limit=8 * 1024 * 1024):
    vmem = pl.BlockSpec(memory_space=pltpu.VMEM)
    return pl.pallas_call(
        body,
        in_specs=[pl.BlockSpec(memory_space=pltpu.SMEM)] + [vmem] * len(args),
        out_specs=[vmem] * len(out_shape),
        out_shape=out_shape,
        compiler_params=pltpu.CompilerParams(vmem_limit_bytes=limit),
        cost_estimate=pl.CostEstimate(
            flops=flops, bytes_accessed=4 * 10**6, transcendentals=0
        ),
    )(scalars, *args)


def chosen(where_ref, step, rows):
    at = where_ref[step]
    block = rows[0][...]
    for m in (1, 2, 3):
        block = jnp.where(at == m, rows[m][...], block)
    return block


def times(block, cols):
    return lax.dot_general(
        block, cols, (((1,), (1,)), ((), ())), preferred_element_type=F32
    )


def product_kernel(where_ref, r0, r1, r2, r3, c1, c2, c3, c4, *outs):
    n = c1.shape[0]
    for step, out_a, out_b in zip((2, 1, 3, 0), outs[::2], outs[1::2], strict=True):
        block = chosen(where_ref, step, (r0, r1, r2, r3))
        own = times(block, r0[...])
        out_a[:, :n] = times(block, c1[...]).astype(out_a.dtype)
        out_a[:, n : 2 * n] = times(block, c2[...]).astype(out_a.dtype)
        out_a[:, 2 * n :] = own[:, : n // 2].astype(out_a.dtype)
        out_b[:, :n] = times(block, c3[...]).astype(out_b.dtype)
        out_b[:, n : 2 * n] = times(block, c4[...]).astype(out_b.dtype)
        out_b[:, 2 * n :] = own[:, n // 2 :].astype(out_b.dtype)


def relay_kernel(_, up_a, far_a, down_b, far_b, out_a, out_b):
    out_a[...] = (up_a[...] + far_a[...].astype(F32)).astype(BF)
    out_b[...] = (down_b[...] + far_b[...].astype(F32)).astype(BF)


def home_kernel(
    place_ref, home_a, up_a, down_a, home_b, up_b, down_b, out_ref, t1, t2, t3, *, scale
):
    n = t1.shape[0]

    def at(k):
        return pl.ds(pl.multiple_of(place_ref[k] * n, 128), n)

    a = (home_a[...] + up_a[...].astype(F32) + down_a[...].astype(F32)) * scale
    b = (home_b[...] + up_b[...].astype(F32) + down_b[...].astype(F32)) * scale
    t1[...] = a[:, :n].astype(BF)
    t2[...] = a[:, n : 2 * n].astype(BF)
    t3[...] = b[:, :n].astype(BF)
    out_ref[:, at(1)] = a[:, :n]
    out_ref[:, at(6)] = a[:, n : 2 * n]
    out_ref[:, at(3)] = b[:, :n]
    out_ref[:, at(4)] = b[:, n : 2 * n]
    out_ref[:, at(0)] = jnp.concatenate([a[:, 2 * n :], b[:, 2 * n :]], axis=1)


def two_terms(value):
    high = value.astype(BF)
    return high, (value - high.astype(F32)).astype(BF)


def inner(left, right):
    return lax.dot_general(left, right, (((0,), (0,)), ((), ())), preferred_element_type=F32)


def outer(left, right):
    return jnp.dot(left, right, preferred_element_type=F32)


def sums_kernel(where_ref, flat_ref, orbit_ref, mine_ref, other_ref, hcore_ref, out_ref, part_ref):
    depth = flat_ref.shape[1]
    tile = mine_ref.shape[1]
    shards = hcore_ref.shape[1] // (2 * tile)
    begins_here = where_ref[0] == 0
    columns = []
    for v in range(shards):
        at = where_ref[1] * shards + v
        mine, other = mine_ref[at], other_ref[at]
        columns.append(jnp.where(begins_here, mine, other))
        columns.append(jnp.where(begins_here, other, mine))
    columns = jnp.concatenate(columns, axis=0)
    high, low = two_terms(hcore_ref[...])
    part = outer(high, columns) + outer(low, columns)
    part_ref[...] = part
    orbit = orbit_ref[...]
    high, low = two_terms(part)
    out_ref[:depth] = inner(flat_ref[...], orbit)
    out_ref[depth:] = inner(orbit, high) + inner(orbit, low)


def spread_kernel(_, pieces_ref, out_ref):
    total = jnp.sum(pieces_ref[...], axis=0)
    out_ref[...] = jnp.broadcast_to(total[None], out_ref.shape)


def applied_kernel(_, flat_ref, summed_ref, part_ref, out_ref, *, factor):
    rows, depth = flat_ref.shape
    high, low = two_terms(summed_ref[:depth])
    flat = flat_ref[...]
    out_ref[:rows] = part_ref[...] - factor * (outer(flat, high) + outer(flat, low))
    out_ref[rows:] = summed_ref[depth:] - factor * (
        inner(high, high) + inner(high, low) + inner(low, high)
    )


def add_kernel(_, left, right, out_ref):
    out_ref[...] = left[...] + right[...]


def gradient_kernel(_, orbit_ref, left, right, out_ref):
    rows = orbit_ref.shape[0]
    high, low = two_terms(left[rows:] + right[rows:])
    orbit = orbit_ref[...]
    out_ref[...] = left[:rows] + right[:rows] - (outer(orbit, high) + outer(orbit, low))


def place_kernel(place_ref, t1, t2, t3, _, out_ref, turned, sems):
    n = t1.shape[0]
    copies = []
    for k, tile in enumerate((t1, t2, t3)):
        turned[k] = tile[...].astype(F32).T
        at = pl.ds(pl.multiple_of(place_ref[8 - OFFSETS[k]] * n, 128), n)
        copies.append(pltpu.make_async_copy(turned.at[k], out_ref.at[:, at], sems.at[k]))
        copies[-1].start()
    for copy in copies:
        copy.wait()


def place(where, tiles, out):
    n = tiles[0].shape[0]
    vmem = pl.BlockSpec(memory_space=pltpu.VMEM)
    hbm = pl.BlockSpec(memory_space=pl.ANY)
    return pl.pallas_call(
        place_kernel,
        in_specs=[pl.BlockSpec(memory_space=pltpu.SMEM)] + [vmem] * 3 + [hbm],
        out_specs=hbm,
        out_shape=jax.ShapeDtypeStruct(out.shape, out.dtype),
        input_output_aliases={4: 0},
        scratch_shapes=[pltpu.VMEM((3, n, n), F32), pltpu.SemaphoreType.DMA((3,))],
        compiler_params=pltpu.CompilerParams(vmem_limit_bytes=VMEM_LIMIT),
    )(where, *tiles, out)


def on_device(slab, screen, orbitals, hcore):
    quantity, row_count, basis = slab.shape
    occupied = orbitals.shape[1]
    depth = quantity * occupied
    core = lax.axis_index("core")
    aux = lax.axis_index(AUX)
    z = lax.axis_index("z")
    plane = lax.axis_index("y") * 2 + lax.axis_index("xl")
    row_devices = lax.axis_size(ROW)
    scale = 1.0 / math.sqrt(quantity * 4 * occupied)

    own = lax.dynamic_slice_in_dim(orbitals, core * (row_count // 2), row_count // 2, 0)
    where = ((z + jnp.arange(4, dtype=jnp.int32)) % 4) ^ aux
    spots = spot((plane + jnp.arange(8, dtype=jnp.int32)) % 8)
    own, here, there, ids, where, spots = lax.optimization_barrier(
        (own, core[None], 1 - core[None], jnp.stack([core, aux]), where, spots)
    )
    mine = lax.all_to_all(
        jnp.broadcast_to(own[None], (row_devices,) + own.shape), ROW, 0, 0, tiled=True
    )
    other = flip(mine, "core", 1, 2)

    kept, begun = half_begin(here, screen[0], slab, mine)
    flat = half_end(there, screen[0], kept, other, begun)

    swapped, far_rows = [
        lax.ppermute(
            flat,
            ("xh", "core", "z"),
            [(a * 4 + k, (k ^ m) * 4 + a) for a in range(4) for k in range(4)],
        )
        for m in (0, 2)
    ]
    swapped, far_rows = lax.optimization_barrier((swapped, far_rows))
    summed, core_part = plain(
        sums_kernel,
        [
            jax.ShapeDtypeStruct((depth + occupied, occupied), F32),
            jax.ShapeDtypeStruct((row_count, occupied), F32),
        ],
        ids,
        flat,
        orbitals,
        mine,
        other,
        hcore,
        flops=10**10,
    )

    columns = [
        lax.ppermute(swapped, PLANE, [(spot((s + m) % 8), spot(s)) for s in range(8)])
        for m in OFFSETS
    ]
    near, far = flip(jnp.stack([swapped, far_rows]), "core", 1, 2)
    factors = [swapped, near, far_rows, far]
    factors += columns
    pieces = summed.reshape(row_devices, -1, occupied)
    pieces = lax.all_to_all(pieces, ROW, 0, 0, tiled=True)
    pieces, factors[4] = lax.optimization_barrier((pieces, factors[4]))
    part = jax.ShapeDtypeStruct((row_count, 5 * row_count // 2), BF)
    part_f32 = jax.ShapeDtypeStruct(part.shape, F32)
    far_a, far_b, up_a, up_b, down_a, down_b, home_a, home_b = plain(
        product_kernel,
        [part, part, part_f32, part, part, part_f32, part_f32, part_f32],
        where,
        *factors,
    )
    (pieces,) = plain(
        spread_kernel,
        [jax.ShapeDtypeStruct(pieces.shape, F32)],
        where,
        pieces,
        flops=10**10,
    )
    far_a = shift(far_a, "z", 1, 4)
    far_b = shift(far_b, "z", -1, 4)
    up_b = shift(up_b, "z", 1, 4)
    down_a = shift(down_a, "z", -1, 4)
    up_a, down_b = plain(relay_kernel, [part, part], where, up_a, far_a, down_b, far_b)
    up_a = shift(up_a, "z", 1, 4)
    down_b = shift(down_b, "z", -1, 4)
    tile = jax.ShapeDtypeStruct((row_count, row_count), BF)
    exchange, *tiles = plain(
        functools.partial(home_kernel, scale=scale),
        [jax.ShapeDtypeStruct(hcore.shape, F32), tile, tile, tile],
        spots,
        home_a,
        up_a,
        down_a,
        home_b,
        up_b,
        down_b,
    )
    turned = [
        lax.ppermute(
            tile,
            AUX + ROW,
            [
                (a * 32 + k * 8 + spot(s), k * 32 + a * 8 + spot((s + m) % 8))
                for a in range(4)
                for k in range(4)
                for s in range(8)
            ],
        )
        for m, tile in zip(OFFSETS, tiles, strict=False)
    ]
    exchange = place(spots, turned, exchange)

    summed = lax.all_to_all(pieces, ROW, 0, 0, tiled=True).reshape(summed.shape)
    (both,) = plain(
        functools.partial(applied_kernel, factor=0.5 * scale),
        [jax.ShapeDtypeStruct((row_count + occupied, occupied), F32)],
        where,
        flat,
        summed,
        core_part,
    )
    (both,) = plain(
        add_kernel,
        [jax.ShapeDtypeStruct(both.shape, F32)],
        where,
        both,
        flip(both, "core", 1, 2),
    )
    (gradient,) = plain(
        gradient_kernel,
        [jax.ShapeDtypeStruct((row_count, occupied), F32)],
        where,
        orbitals,
        both,
        flip(both, "xh", 1, 2),
    )
    return (exchange, gradient)


def solution(mesh):
    finer = Mesh(mesh.devices.reshape(2, 2, 4, 2, 4), AUX + ROW)
    in_specs = (P(AUX, ROW, None), P(AUX, ROW, None), P(ROW, None), P(ROW, AUX))
    out_specs = (P(ROW, AUX), P(ROW, None))
    return jax.shard_map(
        on_device, mesh=finer, in_specs=in_specs, out_specs=out_specs, check_vma=False
    )
```

```python
import functools
import math

import jax
import jax.numpy as jnp
from jax import lax
from jax.experimental import pallas as pl
from jax.experimental.pallas import tpu as pltpu
from jax.sharding import Mesh, PartitionSpec as P

ROW = ("z", "xl", "y")
AUX = ("xh", "core")
PLANE = ("xl", "y")
BF = jnp.bfloat16
F32 = jnp.float32
SHARDS = 8
OFFSETS = (1, 6, 3, 4)
VMEM_LIMIT = 16 * 1024 * 1024


def flip(value, axis, mask, size):
    return lax.ppermute(value, axis, [(k, k ^ mask) for k in range(size)])


def shift(value, axis, step, size):
    return lax.ppermute(value, axis, [(k, (k + step) % size) for k in range(size)])


def spot(s):
    return (s % 2) * 4 + s // 2


def screened(screen_ref, t, orbit_ref, parity, begin):
    return jnp.concatenate(
        [
            orbit_ref[v] * screen_ref[t, 2 * v + parity].astype(F32).astype(BF)
            for v in range(begin, begin + SHARDS)
        ],
        axis=0,
    )


def one_chunk(parity, screen_ref, slab_ref, orbit_ref, t, begin):
    quantity = slab_ref.shape[0]
    tile = orbit_ref.shape[1]
    block = jnp.concatenate(
        [
            slab_ref[
                :,
                t * tile : (t + 1) * tile,
                pl.ds(pl.multiple_of((2 * v + parity) * tile, tile), tile),
            ].reshape(quantity * tile, tile)
            for v in range(begin, begin + SHARDS)
        ],
        axis=1,
    )
    return jnp.dot(
        block,
        screened(screen_ref, t, orbit_ref, parity, begin),
        preferred_element_type=F32,
    )


def begin_kernel(parity_ref, screen_ref, slab_ref, orbit_ref, kept_ref, out_ref, sems):
    quantity, rows, _ = kept_ref.shape
    shards, tile, _ = orbit_ref.shape
    groups = rows // tile
    width = 2 * SHARDS * tile
    chunks = shards // SHARDS
    copies = [
        pltpu.make_async_copy(
            slab_ref.at[:, :, pl.ds(c * width, width)],
            kept_ref.at[:, :, pl.ds(c * width, width)],
            sems.at[c],
        )
        for c in range(chunks)
    ]
    copies[0].start()
    copies[1].start()
    for c in range(chunks):
        copies[c].wait()
        if c + 2 < chunks:
            copies[c + 2].start()
        for t in range(groups):
            term = one_chunk(
                parity_ref[0], screen_ref, kept_ref, orbit_ref, t, c * SHARDS
            )
            out_ref[t] = term if c == 0 else out_ref[t] + term


def end_kernel(parity_ref, screen_ref, kept_ref, orbit_ref, begun_ref, out_ref):
    quantity, rows, _ = kept_ref.shape
    tile = orbit_ref.shape[1]
    for t in range(rows // tile):
        total = begun_ref[t]
        for begin in range(0, orbit_ref.shape[0], SHARDS):
            total = total + one_chunk(
                parity_ref[0], screen_ref, kept_ref, orbit_ref, t, begin
            )
        for q in range(quantity):
            out_ref[t * tile : (t + 1) * tile, q * tile : (q + 1) * tile] = total[
                q * tile : (q + 1) * tile
            ].astype(BF)


def half_begin(parity, screen, slab, orbit):
    quantity, rows, _ = slab.shape
    _, tile, occupied = orbit.shape
    groups = rows // tile
    vmem = pl.BlockSpec(memory_space=pltpu.VMEM)
    smem = pl.BlockSpec(memory_space=pltpu.SMEM)
    return pl.pallas_call(
        begin_kernel,
        in_specs=[smem, smem, pl.BlockSpec(memory_space=pl.ANY), vmem],
        out_specs=[vmem, vmem],
        out_shape=[
            jax.ShapeDtypeStruct(slab.shape, BF),
            jax.ShapeDtypeStruct((groups, quantity * tile, occupied), F32),
        ],
        scratch_shapes=[pltpu.SemaphoreType.DMA((orbit.shape[0] // SHARDS,))],
        compiler_params=pltpu.CompilerParams(vmem_limit_bytes=VMEM_LIMIT),
        cost_estimate=pl.CostEstimate(
            flops=slab.size * occupied, bytes_accessed=2 * slab.size, transcendentals=0
        ),
    )(parity, screen, slab, orbit)


def half_end(parity, screen, kept, orbit, begun):
    quantity, rows, _ = kept.shape
    vmem = pl.BlockSpec(memory_space=pltpu.VMEM)
    smem = pl.BlockSpec(memory_space=pltpu.SMEM)
    return pl.pallas_call(
        end_kernel,
        in_specs=[smem, smem, vmem, vmem, vmem],
        out_specs=vmem,
        out_shape=jax.ShapeDtypeStruct((rows, quantity * orbit.shape[2]), BF),
        compiler_params=pltpu.CompilerParams(vmem_limit_bytes=VMEM_LIMIT),
        cost_estimate=pl.CostEstimate(
            flops=kept.size * orbit.shape[2], bytes_accessed=kept.size, transcendentals=0
        ),
    )(parity, screen, kept, orbit, begun)


def plain(body, out_shape, scalars, *args, flops=10**9, limit=8 * 1024 * 1024):
    vmem = pl.BlockSpec(memory_space=pltpu.VMEM)
    return pl.pallas_call(
        body,
        in_specs=[pl.BlockSpec(memory_space=pltpu.SMEM)] + [vmem] * len(args),
        out_specs=[vmem] * len(out_shape),
        out_shape=out_shape,
        compiler_params=pltpu.CompilerParams(vmem_limit_bytes=limit),
        cost_estimate=pl.CostEstimate(
            flops=flops, bytes_accessed=4 * 10**6, transcendentals=0
        ),
    )(scalars, *args)


def chosen(where_ref, step, rows):
    at = where_ref[step]
    block = rows[0][...]
    for m in (1, 2, 3):
        block = jnp.where(at == m, rows[m][...], block)
    return block


def times(block, cols):
    return lax.dot_general(
        block, cols, (((1,), (1,)), ((), ())), preferred_element_type=F32
    )


def product_kernel(where_ref, r0, r1, r2, r3, c1, c2, c3, c4, *outs):
    n = c1.shape[0]
    for step, out_a, out_b in zip((2, 1, 3, 0), outs[::2], outs[1::2], strict=True):
        block = chosen(where_ref, step, (r0, r1, r2, r3))
        own = times(block, r0[...])
        out_a[:, :n] = times(block, c1[...]).astype(out_a.dtype)
        out_a[:, n : 2 * n] = times(block, c2[...]).astype(out_a.dtype)
        out_a[:, 2 * n :] = own[:, : n // 2].astype(out_a.dtype)
        out_b[:, :n] = times(block, c3[...]).astype(out_b.dtype)
        out_b[:, n : 2 * n] = times(block, c4[...]).astype(out_b.dtype)
        out_b[:, 2 * n :] = own[:, n // 2 :].astype(out_b.dtype)


def relay_kernel(_, up_a, far_a, down_b, far_b, out_a, out_b):
    out_a[...] = (up_a[...].astype(F32) + far_a[...].astype(F32)).astype(BF)
    out_b[...] = (down_b[...].astype(F32) + far_b[...].astype(F32)).astype(BF)


def home_kernel(
    place_ref, home_a, up_a, down_a, home_b, up_b, down_b, out_ref, t1, t2, t3, *, scale
):
    n = t1.shape[0]

    def at(k):
        return pl.ds(pl.multiple_of(place_ref[k] * n, 128), n)

    a = (home_a[...].astype(F32) + up_a[...].astype(F32) + down_a[...].astype(F32)) * scale
    b = (home_b[...].astype(F32) + up_b[...].astype(F32) + down_b[...].astype(F32)) * scale
    t1[...] = a[:, :n].astype(BF)
    t2[...] = a[:, n : 2 * n].astype(BF)
    t3[...] = b[:, :n].astype(BF)
    out_ref[:, at(1)] = a[:, :n]
    out_ref[:, at(6)] = a[:, n : 2 * n]
    out_ref[:, at(3)] = b[:, :n]
    out_ref[:, at(4)] = b[:, n : 2 * n]
    out_ref[:, at(0)] = jnp.concatenate([a[:, 2 * n :], b[:, 2 * n :]], axis=1)


def two_terms(value):
    high = value.astype(BF)
    return high, (value - high.astype(F32)).astype(BF)


def inner(left, right):
    return lax.dot_general(left, right, (((0,), (0,)), ((), ())), preferred_element_type=F32)


def outer(left, right):
    return jnp.dot(left, right, preferred_element_type=F32)


def sums_kernel(where_ref, flat_ref, orbit_ref, mine_ref, other_ref, hcore_ref, out_ref, part_ref):
    depth = flat_ref.shape[1]
    tile = mine_ref.shape[1]
    shards = hcore_ref.shape[1] // (2 * tile)
    begins_here = where_ref[0] == 0
    columns = []
    for v in range(shards):
        at = where_ref[1] * shards + v
        mine, other = mine_ref[at], other_ref[at]
        columns.append(jnp.where(begins_here, mine, other))
        columns.append(jnp.where(begins_here, other, mine))
    columns = jnp.concatenate(columns, axis=0)
    high, low = two_terms(hcore_ref[...])
    part = outer(high, columns) + outer(low, columns)
    part_ref[...] = part
    orbit = orbit_ref[...]
    high, low = two_terms(part)
    out_ref[:depth] = inner(flat_ref[...], orbit)
    out_ref[depth:] = inner(orbit, high) + inner(orbit, low)


def spread_kernel(_, pieces_ref, out_ref):
    total = jnp.sum(pieces_ref[...], axis=0)
    out_ref[...] = jnp.broadcast_to(total[None], out_ref.shape)


def applied_kernel(_, flat_ref, summed_ref, part_ref, out_ref, *, factor):
    rows, depth = flat_ref.shape
    high, low = two_terms(summed_ref[:depth])
    flat = flat_ref[...]
    out_ref[:rows] = part_ref[...] - factor * (outer(flat, high) + outer(flat, low))
    out_ref[rows:] = summed_ref[depth:] - factor * (
        inner(high, high) + inner(high, low) + inner(low, high)
    )


def add_kernel(_, left, right, out_ref):
    out_ref[...] = left[...] + right[...]


def gradient_kernel(_, orbit_ref, left, right, out_ref):
    rows = orbit_ref.shape[0]
    high, low = two_terms(left[rows:] + right[rows:])
    orbit = orbit_ref[...]
    out_ref[...] = left[:rows] + right[:rows] - (outer(orbit, high) + outer(orbit, low))


def place_kernel(place_ref, t1, t2, t3, _, out_ref, turned, sems):
    n = t1.shape[0]
    copies = []
    for k, tile in enumerate((t1, t2, t3)):
        turned[k] = tile[...].astype(F32).T
        at = pl.ds(pl.multiple_of(place_ref[8 - OFFSETS[k]] * n, 128), n)
        copies.append(pltpu.make_async_copy(turned.at[k], out_ref.at[:, at], sems.at[k]))
        copies[-1].start()
    for copy in copies:
        copy.wait()


def place(where, tiles, out):
    n = tiles[0].shape[0]
    vmem = pl.BlockSpec(memory_space=pltpu.VMEM)
    hbm = pl.BlockSpec(memory_space=pl.ANY)
    return pl.pallas_call(
        place_kernel,
        in_specs=[pl.BlockSpec(memory_space=pltpu.SMEM)] + [vmem] * 3 + [hbm],
        out_specs=hbm,
        out_shape=jax.ShapeDtypeStruct(out.shape, out.dtype),
        input_output_aliases={4: 0},
        scratch_shapes=[pltpu.VMEM((3, n, n), F32), pltpu.SemaphoreType.DMA((3,))],
        compiler_params=pltpu.CompilerParams(vmem_limit_bytes=VMEM_LIMIT),
    )(where, *tiles, out)


def on_device(slab, screen, orbitals, hcore):
    quantity, row_count, basis = slab.shape
    occupied = orbitals.shape[1]
    depth = quantity * occupied
    core = lax.axis_index("core")
    aux = lax.axis_index(AUX)
    z = lax.axis_index("z")
    plane = lax.axis_index("y") * 2 + lax.axis_index("xl")
    row_devices = lax.axis_size(ROW)
    scale = 1.0 / math.sqrt(quantity * 4 * occupied)

    own = lax.dynamic_slice_in_dim(orbitals, core * (row_count // 2), row_count // 2, 0)
    where = ((z + jnp.arange(4, dtype=jnp.int32)) % 4) ^ aux
    spots = spot((plane + jnp.arange(8, dtype=jnp.int32)) % 8)
    own, here, there, ids, where, spots = lax.optimization_barrier(
        (own, core[None], 1 - core[None], jnp.stack([core, aux]), where, spots)
    )
    mine = lax.all_to_all(
        jnp.broadcast_to(own[None], (row_devices,) + own.shape), ROW, 0, 0, tiled=True
    )
    other = flip(mine, "core", 1, 2)

    kept, begun = half_begin(here, screen[0], slab, mine)
    flat = half_end(there, screen[0], kept, other, begun)

    swapped, far_rows = [
        lax.ppermute(
            flat,
            ("xh", "core", "z"),
            [(a * 4 + k, (k ^ m) * 4 + a) for a in range(4) for k in range(4)],
        )
        for m in (0, 2)
    ]
    swapped, far_rows = lax.optimization_barrier((swapped, far_rows))
    summed, core_part = plain(
        sums_kernel,
        [
            jax.ShapeDtypeStruct((depth + occupied, occupied), F32),
            jax.ShapeDtypeStruct((row_count, occupied), F32),
        ],
        ids,
        flat,
        orbitals,
        mine,
        other,
        hcore,
        flops=10**10,
    )

    columns = [
        lax.ppermute(swapped, PLANE, [(spot((s + m) % 8), spot(s)) for s in range(8)])
        for m in OFFSETS
    ]
    near, far = flip(jnp.stack([swapped, far_rows]), "core", 1, 2)
    factors = [swapped, near, far_rows, far]
    factors += columns
    pieces = summed.reshape(row_devices, -1, occupied)
    pieces = lax.all_to_all(pieces, ROW, 0, 0, tiled=True)
    pieces, factors[4] = lax.optimization_barrier((pieces, factors[4]))
    part = jax.ShapeDtypeStruct((row_count, 5 * row_count // 2), BF)
    far_a, far_b, up_a, up_b, down_a, down_b, home_a, home_b = plain(
        product_kernel,
        [part] * 8,
        where,
        *factors,
    )
    (pieces,) = plain(
        spread_kernel,
        [jax.ShapeDtypeStruct(pieces.shape, F32)],
        where,
        pieces,
        flops=10**10,
    )
    far_a = shift(far_a, "z", 1, 4)
    far_b = shift(far_b, "z", -1, 4)
    up_b = shift(up_b, "z", 1, 4)
    down_a = shift(down_a, "z", -1, 4)
    up_a, down_b = plain(relay_kernel, [part, part], where, up_a, far_a, down_b, far_b)
    up_a = shift(up_a, "z", 1, 4)
    down_b = shift(down_b, "z", -1, 4)
    tile = jax.ShapeDtypeStruct((row_count, row_count), BF)
    exchange, *tiles = plain(
        functools.partial(home_kernel, scale=scale),
        [jax.ShapeDtypeStruct(hcore.shape, F32), tile, tile, tile],
        spots,
        home_a,
        up_a,
        down_a,
        home_b,
        up_b,
        down_b,
    )
    turned = [
        lax.ppermute(
            tile,
            AUX + ROW,
            [
                (a * 32 + k * 8 + spot(s), k * 32 + a * 8 + spot((s + m) % 8))
                for a in range(4)
                for k in range(4)
                for s in range(8)
            ],
        )
        for m, tile in zip(OFFSETS, tiles, strict=False)
    ]
    exchange = place(spots, turned, exchange)

    summed = lax.all_to_all(pieces, ROW, 0, 0, tiled=True).reshape(summed.shape)
    (both,) = plain(
        functools.partial(applied_kernel, factor=0.5 * scale),
        [jax.ShapeDtypeStruct((row_count + occupied, occupied), F32)],
        where,
        flat,
        summed,
        core_part,
    )
    (both,) = plain(
        add_kernel,
        [jax.ShapeDtypeStruct(both.shape, F32)],
        where,
        both,
        flip(both, "core", 1, 2),
    )
    (gradient,) = plain(
        gradient_kernel,
        [jax.ShapeDtypeStruct((row_count, occupied), F32)],
        where,
        orbitals,
        both,
        flip(both, "xh", 1, 2),
    )
    return (exchange, gradient)


def solution(mesh):
    finer = Mesh(mesh.devices.reshape(2, 2, 4, 2, 4), AUX + ROW)
    in_specs = (P(AUX, ROW, None), P(AUX, ROW, None), P(ROW, None), P(ROW, AUX))
    out_specs = (P(ROW, AUX), P(ROW, None))
    return jax.shard_map(
        on_device, mesh=finer, in_specs=in_specs, out_specs=out_specs, check_vma=False
    )
```
